32 devices in a mesh: grp: 2 (over x), aux: 8 (over z, y), pair: 2 (over core).
Axes of the slice: x: 2, y: 2, z: 4, core: 2. Of those that a mesh axis runs over, the one named last changes fastest.
Arguments:
- integrals: float32 [512, 384, 384], P(('grp', 'aux'), 'pair'), parts along dimension 0, may hold values from -6 to 6
- coef: float32 [384, 256], replicated, may hold values from -0.3125 to 0.3125
- screen: int32 [6, 6], replicated, may hold values 0 or 1
- domains: int32 [256, 128], replicated, may hold values from 0 to 255, all different within a row
- owner: int32 [32768], replicated, may hold values from 0 to 32767, each once
- metric: float32 [512, 256], P(('grp', 'aux'), 'pair'), parts along dimension 0, may hold values from -0.375 to 0.375
Outputs:
- fitted: float32 [512, 32768], P('grp', ('aux', 'pair')), parts along dimension 0
The draws below stay inside these ranges and needn't reach their ends.
There are 2 independent parts, one for each index of `grp`. The reference program is written for one: setup_inputs(seed, part) draws one part's arguments, and reference() takes and returns one part's arrays. A program takes and returns all parts, laid end to end along the dimension named above; an argument that names none is the same for every part. Nothing has to cross between parts.
Inputs may be any that keep to these rules, and one draw needn't show every extreme that they name: `domains`: each row names distinct orbitals and every orbital is named by some row. `owner`: each pair appears once.
All inputs are finite; a program needn't handle non-finite values.
Results may differ from the reference program's by a relative error of at most 0.000071.
Values sent between devices are 32-bit elements; how exact they have to be, the bound alone decides.
A program may use at most 192 MiB of HBM per device.

```python
import jax
import jax.numpy as jnp
from jax import lax

NOCC = 256
NBLK = 6
DOM = 128
NB = 384
AUX = 256
NPAIR = 32768


def place_ends(entries, stream_key, least, largest):
    place = [jax.random.randint(jax.random.fold_in(stream_key, axis), (), 0, length) for axis, length in enumerate(entries.shape)]
    longest = entries.shape.index(max(entries.shape))
    neighbour = place[:longest] + [(place[longest] + 1) % entries.shape[longest]] + place[longest + 1:]
    return entries.at[tuple(place)].set(least).at[tuple(neighbour)].set(largest)


def block_scale(stream_key, extent, pieces, smallest, largest):
    level = 1.0
    for axis_at, parts in pieces:
        steps = jax.random.uniform(jax.random.fold_in(jax.random.fold_in(stream_key, 6), axis_at), (parts,), jnp.float32, smallest / len(pieces), largest / len(pieces))
        level = level * jnp.repeat(jnp.exp(steps), extent[axis_at] // parts).reshape((-1,) + (1,) * (len(extent) - 1 - axis_at))
    return level


def picks_of(key, rows, amount, top, lift):
    ranking = jax.random.permutation(jax.random.fold_in(key, 1), amount)
    boost = ranking
    for power in range(3):
        boost = boost * boost // amount
    boost = boost * lift // amount
    lots = jax.random.randint(jax.random.fold_in(key, 2), (rows, amount), 0, 4096) + boost
    sure = jax.random.permutation(jax.random.fold_in(key, 3), rows)[jnp.arange(amount) % rows]
    lots = jnp.where(jnp.arange(rows)[:, None] == sure[None, :], 1 << 14, lots)
    score = lots * amount + jnp.arange(amount)
    return lax.top_k(score.astype(jnp.int32), top)[1].astype(jnp.int32)


def noise(own_key, extent, width, limit, pieces=(), dtype=jnp.bfloat16):
    values = jax.random.normal(own_key, extent, jnp.float32) * width
    if len(pieces) > 0:
        values = block_scale(own_key, extent, pieces, -0.22, 0.18) * values
    return jnp.clip(values, min=-limit, max=limit).astype(dtype)


def setup_inputs(seed: int = 0, part: int = 0) -> dict:
    keys = jax.random.split(jax.random.key(seed), 7)
    own_keys = jax.random.split(jax.random.fold_in(keys[6], part), 7)
    return {
        "integrals": noise(own_keys[0], (AUX, NB, NB), 1.0, 6.0, ((0, 8), (1, 2)), jnp.float32),
        "coef": noise(keys[1], (NB, NOCC), NB ** -0.5, 0.3125, (), jnp.float32),
        "screen": place_ends((jax.random.randint(keys[2], (NBLK, NBLK), 0, 4) < 3).astype(jnp.int32), jax.random.fold_in(keys[2], 1), 0, 1),
        "domains": picks_of(keys[3], NOCC, NOCC, DOM, 4096),
        "owner": jax.random.permutation(keys[4], NPAIR).astype(jnp.int32),
        "metric": noise(own_keys[5], (AUX, AUX), AUX ** -0.5, 0.375, ((0, 8), (1, 2)), jnp.float32),
    }


def reference(integrals, coef, screen, domains, owner, metric):
    blocks = screen.astype(jnp.float32)
    expanded = jnp.repeat(jnp.repeat(blocks, 64, axis=0), 64, axis=1)
    masked = integrals * expanded[None]
    half_ints = jnp.einsum("pmn,ni->pmi", masked, coef, precision=lax.Precision.HIGHEST)
    quarter = jnp.einsum("mi,pmj->pij", coef, half_ints, precision=lax.Precision.HIGHEST)
    occ_first = owner // DOM
    occ_second = domains[occ_first, owner % DOM]
    flat_index = (occ_first * NOCC + occ_second).astype(jnp.int32)
    chosen = jnp.take(quarter.reshape(quarter.shape[0], NOCC * NOCC), flat_index, axis=1)
    return jnp.dot(metric, chosen, precision=lax.Precision.HIGHEST, preferred_element_type=jnp.float32)
```

```python
import functools

import jax
import jax.numpy as jnp
from jax import lax
from jax.experimental import pallas as pl
from jax.experimental.pallas import tpu as pltpu
from jax.sharding import PartitionSpec as P

MESH = pl.DeviceIdType.MESH
LANES = 128
VMEM_LIMIT = 60 * 1024 * 1024


def split2(x):
    hi = x.astype(jnp.bfloat16)
    lo = (x - hi.astype(jnp.float32)).astype(jnp.bfloat16)
    return hi, lo


def dot3(a, b, dims=(((1,), (0,)), ((), ()))):
    (ah, al), (bh, bl) = a, b
    mm = functools.partial(lax.dot_general, dimension_numbers=dims, preferred_element_type=jnp.float32)
    return mm(ah, bh) + (mm(ah, bl) + mm(al, bh))


def spread(x, lane):
    quarter = LANES // 4
    group = lane // quarter
    odd = (group % 2) == 1
    high = group >= 2
    even_pair = jnp.where(odd, pltpu.roll(x, quarter, 1), x)
    odd_pair = jnp.where(odd, x, pltpu.roll(x, LANES - quarter, 1))
    even_far = pltpu.roll(even_pair, 2 * quarter, 1)
    odd_far = pltpu.roll(odd_pair, 2 * quarter, 1)
    return (
        jnp.where(high, even_far, even_pair),
        jnp.where(high, odd_far, odd_pair),
        jnp.where(high, even_pair, even_far),
        jnp.where(high, odd_pair, odd_far),
    )


def transform_kernel(
    integrals_ref, mask_ref, coef_ref, coef_t_ref, rows_ref, owner_ref, out_ref,
    ibuf, coef_hl, coef_t_hl, t0, t1, table, sems,
):
    aux_loc, mu_loc, nb = integrals_ref.shape
    nocc = coef_ref.shape[1]
    dests, rows_per, _ = out_ref.shape

    def fetch(p, slot):
        return pltpu.make_async_copy(integrals_ref.at[p], ibuf.at[slot], sems.at[slot])

    fetch(0, 0).start()
    coef_hl[0], coef_hl[1] = split2(coef_ref[...])
    coef_t_hl[0], coef_t_hl[1] = split2(coef_t_ref[...])

    def one_p(p, carry):
        slot = lax.rem(p, 2)

        @pl.when(p + 1 < aux_loc)
        def _():
            fetch(p + 1, 1 - slot).start()

        fetch(p, slot).wait()
        x = split2(ibuf[slot] * mask_ref[...])
        half = split2(dot3(x, (coef_hl[0], coef_hl[1])))
        q = dot3((coef_t_hl[0], coef_t_hl[1]), half)
        t0[pl.ds(p, nocc, stride=aux_loc), :] = q[:, :LANES]
        t1[pl.ds(p, nocc, stride=aux_loc), :] = q[:, LANES:]
        return carry

    lax.fori_loop(0, aux_loc, one_p, 0)

    lane = lax.broadcasted_iota(jnp.int32, (LANES, LANES), 1)

    def one_block(ib, carry):
        for jb, t in enumerate((t0, t1)):
            block = t[pl.ds(pl.multiple_of(ib * LANES, LANES), LANES), :].T
            for g, rep in enumerate(spread(block, lane)):
                at = pl.multiple_of((4 * ib + g) * nocc + jb * LANES, LANES)
                table[pl.ds(at, LANES), :] = rep
        return carry

    lax.fori_loop(0, nocc // 4, one_block, 0)

    row_lane = lax.broadcasted_iota(jnp.int32, (1, LANES), 1) // (LANES // 4)

    for d in range(dests):
        base = d * rows_per * 4

        def eight(rb, carry, d=d, base=base):
            for u in range(8):
                r = rb * 8 + u
                got = [
                    table[pl.ds(rows_ref[owner_ref[base + g * rows_per + r]], 1), :]
                    for g in range(4)
                ]
                low = jnp.where(row_lane == 0, got[0], got[1])
                high = jnp.where(row_lane == 2, got[2], got[3])
                out_ref[d, pl.ds(r, 1), :] = jnp.where(row_lane < 2, low, high)
            return carry

        lax.fori_loop(0, rows_per // 8, eight, 0)


def exchange_kernel(
    n_aux, part_ref, metric_ref, out_ref, pbuf, snd, rcv, mfull,
    psend, precv, asend, arecv, msend, mrecv,
):
    me_a = lax.axis_index("aux")
    me_c = lax.axis_index("pair")
    n_dev = 2 * n_aux
    me = 2 * me_a + me_c
    q_loc = metric_ref.shape[0]
    rows_per = rcv.shape[1]
    barrier = pltpu.get_barrier_semaphore()

    def greet(k, carry):
        to = lax.rem(me + k, n_dev)
        pl.semaphore_signal(barrier, inc=1, device_id={"aux": to // 2, "pair": to % 2}, device_id_type=MESH)
        return carry

    lax.fori_loop(1, n_dev, greet, 0)
    pl.semaphore_wait(barrier, n_dev - 1)

    def pair_copy(t):
        a = lax.rem(me_a + t, n_aux)
        return pltpu.make_async_remote_copy(
            src_ref=part_ref.at[2 * a + (1 - me_c)], dst_ref=pbuf.at[a],
            send_sem=psend.at[t], recv_sem=precv.at[t],
            device_id={"pair": 1 - me_c}, device_id_type=MESH)

    def metric_copy(k, origin):
        to = lax.rem(me + k, n_dev)
        return pltpu.make_async_remote_copy(
            src_ref=metric_ref,
            dst_ref=mfull.at[origin % 2, pl.ds(pl.multiple_of((origin // 2) * q_loc, q_loc), q_loc), :],
            send_sem=msend.at[k], recv_sem=mrecv.at[k],
            device_id={"aux": to // 2, "pair": to % 2}, device_id_type=MESH)

    def aux_copy(t, origin):
        a = lax.rem(me_a + t, n_aux)
        return pltpu.make_async_remote_copy(
            src_ref=snd.at[a], dst_ref=rcv.at[origin],
            send_sem=asend.at[t], recv_sem=arecv.at[t],
            device_id={"aux": a}, device_id_type=MESH)

    def step(f):
        def g(t, carry):
            f(t)
            return carry
        return g

    lax.fori_loop(1, n_aux, step(lambda t: pair_copy(t).start()), 0)
    pair_copy(0).start()

    def send(t):
        pair_copy(t).wait_recv()
        a = lax.rem(me_a + t, n_aux)
        snd[a] = part_ref[2 * a + me_c] + pbuf[a]
        aux_copy(t, me_a).start()

    lax.fori_loop(1, n_aux, step(send), 0)
    lax.fori_loop(1, n_dev, step(lambda k: metric_copy(k, me).start()), 0)
    pair_copy(0).wait_recv()
    rcv[me_a] = part_ref[2 * me_a + me_c] + pbuf[me_a]
    mfull[me_c, pl.ds(pl.multiple_of(me_a * q_loc, q_loc), q_loc), :] = metric_ref[...]

    lax.fori_loop(1, n_dev, step(lambda k: metric_copy(k, lax.rem(me + n_dev - k, n_dev)).wait_recv()), 0)
    lax.fori_loop(1, n_aux, step(lambda t: aux_copy(t, lax.rem(me_a + n_aux - t, n_aux)).wait_recv()), 0)

    quarter = LANES // 4
    lane_group = lax.broadcasted_iota(jnp.int32, (rows_per, LANES), 1) // quarter
    blocks = n_aux // 4
    for g in range(4):
        acc = None
        for b in range(blocks):
            y = None
            for u in range(4):
                x = rcv[4 * b + u]
                shift = (quarter * (u - g)) % LANES
                x = pltpu.roll(x, shift, 1) if shift else x
                y = x if y is None else jnp.where(lane_group == u, x, y)
            per = blocks // 2
            m = mfull_columns(mfull, b, per)
            add = dot3(split2(m), split2(y), (((1,), (1,)), ((), ())))
            acc = add if acc is None else acc + add
        out_ref[:, g * rows_per:(g + 1) * rows_per] = acc

    lax.fori_loop(0, n_aux, step(lambda t: pair_copy(t).wait_send()), 0)
    lax.fori_loop(1, n_aux, step(lambda t: aux_copy(t, me_a).wait_send()), 0)
    lax.fori_loop(1, n_dev, step(lambda k: metric_copy(k, me).wait_send()), 0)


def mfull_columns(mfull, b, per):
    at = (b % per) * LANES
    return mfull[b // per, :, at:at + LANES]


def body(integrals, coef, screen, domains, owner, metric):
    aux_loc, mu_loc, nb = integrals.shape
    nocc = coef.shape[1]
    dom = domains.shape[1]
    core = lax.axis_index("pair")
    n_aux = lax.axis_size("aux")
    dests = 2 * n_aux
    slots = owner.shape[0] // dests
    rows_per = slots // 4
    q_all = metric.shape[0] * n_aux
    block = nb // screen.shape[0]

    kept = jnp.repeat(screen.astype(jnp.float32), block, axis=0)
    kept = lax.dynamic_slice_in_dim(kept, core * mu_loc, mu_loc, 0)
    mask = jnp.repeat(kept, block, axis=1)
    coef_t = lax.dynamic_slice_in_dim(coef, core * mu_loc, mu_loc, 0).T
    rows = (domains + nocc * lax.broadcasted_iota(jnp.int32, domains.shape, 0)).reshape(-1)

    vm = pl.BlockSpec(memory_space=pltpu.VMEM)
    sm = pl.BlockSpec(memory_space=pltpu.SMEM)
    hbm = pl.BlockSpec(memory_space=pl.ANY)
    part = pl.pallas_call(
        transform_kernel,
        out_shape=jax.ShapeDtypeStruct((dests, rows_per, LANES), jnp.float32),
        in_specs=[hbm, vm, vm, vm, sm, sm],
        out_specs=vm,
        scratch_shapes=[
            pltpu.VMEM((2, mu_loc, nb), jnp.float32),
            pltpu.VMEM((2, nb, nocc), jnp.bfloat16),
            pltpu.VMEM((2, nocc, mu_loc), jnp.bfloat16),
            pltpu.VMEM((nocc * aux_loc, LANES), jnp.float32),
            pltpu.VMEM((nocc * aux_loc, LANES), jnp.float32),
            pltpu.VMEM((nocc * nocc, LANES), jnp.float32),
            pltpu.SemaphoreType.DMA((2,)),
        ],
        compiler_params=pltpu.CompilerParams(vmem_limit_bytes=VMEM_LIMIT),
        name="transform",
    )(integrals, mask, coef, coef_t, rows, owner)

    return pl.pallas_call(
        functools.partial(exchange_kernel, n_aux),
        out_shape=jax.ShapeDtypeStruct((q_all, slots), jnp.float32),
        in_specs=[vm, vm],
        out_specs=vm,
        scratch_shapes=[
            pltpu.VMEM((n_aux, rows_per, LANES), jnp.float32),
            pltpu.VMEM((n_aux, rows_per, LANES), jnp.float32),
            pltpu.VMEM((n_aux, rows_per, LANES), jnp.float32),
            pltpu.VMEM((2, q_all, metric.shape[1]), jnp.float32),
            pltpu.SemaphoreType.DMA((n_aux,)),
            pltpu.SemaphoreType.DMA((n_aux,)),
            pltpu.SemaphoreType.DMA((n_aux,)),
            pltpu.SemaphoreType.DMA((n_aux,)),
            pltpu.SemaphoreType.DMA((dests,)),
            pltpu.SemaphoreType.DMA((dests,)),
        ],
        compiler_params=pltpu.CompilerParams(
            vmem_limit_bytes=VMEM_LIMIT, collective_id=0, has_side_effects=True),
        name="exchange",
    )(part, metric)


def solution(mesh):
    placed = (P(("grp", "aux"), "pair", None), P(), P(), P(), P(), P(("grp", "aux"), "pair"))
    return jax.shard_map(
        body, mesh=mesh, in_specs=placed, out_specs=P("grp", ("aux", "pair")), check_vma=False
    )
```

```python
import functools

import jax
import jax.numpy as jnp
from jax import lax
from jax.experimental import pallas as pl
from jax.experimental.pallas import tpu as pltpu
from jax.sharding import PartitionSpec as P

MESH = pl.DeviceIdType.MESH
LANES = 128
BATCH = 4
VMEM_LIMIT = 62 * 1024 * 1024


def split2(x):
    hi = x.astype(jnp.bfloat16)
    lo = (x - hi.astype(jnp.float32)).astype(jnp.bfloat16)
    return hi, lo


def dot3(a, b, dims=(((1,), (0,)), ((), ()))):
    (ah, al), (bh, bl) = a, b
    mm = functools.partial(lax.dot_general, dimension_numbers=dims, preferred_element_type=jnp.float32)
    return mm(ah, bh) + (mm(ah, bl) + mm(al, bh))


def spread(x, lane):
    quarter = LANES // 4
    group = lane // quarter
    odd = (group % 2) == 1
    high = group >= 2
    even_pair = jnp.where(odd, pltpu.roll(x, quarter, 1), x)
    odd_pair = jnp.where(odd, x, pltpu.roll(x, LANES - quarter, 1))
    even_far = pltpu.roll(even_pair, 2 * quarter, 1)
    odd_far = pltpu.roll(odd_pair, 2 * quarter, 1)
    return (
        jnp.where(high, even_far, even_pair),
        jnp.where(high, odd_far, odd_pair),
        jnp.where(high, even_pair, even_far),
        jnp.where(high, odd_pair, odd_far),
    )


def fused_kernel(
    n_aux, integrals_ref, screen_ref, coef_ref, rows_ref, owner_ref, metric_ref, out_ref,
    ibuf, mask, coef_hl, coef_t_hl, t0, t1, table, pairs, pbuf, snd, rcv, mfull,
    sems, psend, precv, asend, arecv, msend, mrecv,
):
    aux_loc, mu_loc, nb = integrals_ref.shape
    nocc = coef_ref.shape[1]
    batch = ibuf.shape[1]
    q_loc = metric_ref.shape[0]
    rows_per = rcv.shape[1]
    n_dev = 2 * n_aux
    me_a = lax.axis_index("aux")
    me_c = lax.axis_index("pair")
    me = 2 * me_a + me_c
    quarter = LANES // 4

    def step(f):
        def g(t, carry):
            f(t)
            return carry
        return g

    barrier = pltpu.get_barrier_semaphore()

    def greet(k):
        to = lax.rem(me + k, n_dev)
        pl.semaphore_signal(barrier, inc=1, device_id={"aux": to // 2, "pair": to % 2}, device_id_type=MESH)

    lax.fori_loop(1, n_dev, step(greet), 0)

    def fetch(p, slot):
        return pltpu.make_async_copy(integrals_ref.at[pl.ds(p * batch, batch)], ibuf.at[slot], sems.at[slot])

    fetch(0, 0).start()
    coef_hl[0], coef_hl[1] = split2(coef_ref[...])
    coef_t = coef_ref[pl.ds(pl.multiple_of(me_c * mu_loc, 64), mu_loc), :].T
    coef_t_hl[0], coef_t_hl[1] = split2(coef_t)
    n_blk = screen_ref.shape[0]
    width = nb // n_blk
    lane_blk = lax.broadcasted_iota(jnp.int32, (width, nb), 1) // width
    for rb in range(mu_loc // width):
        line = jnp.zeros((width, nb), jnp.float32)
        for cb in range(n_blk):
            kept = screen_ref[me_c * (mu_loc // width) + rb, cb].astype(jnp.float32)
            line = jnp.where(lane_blk == cb, kept, line)
        mask[rb * width:(rb + 1) * width, :] = line

    n_steps = aux_loc // batch

    def one_step(p, carry):
        slot = lax.rem(p, 2)

        @pl.when(p + 1 < n_steps)
        def _():
            fetch(p + 1, 1 - slot).start()

        fetch(p, slot).wait()
        x = split2((ibuf[slot] * mask[...][None]).reshape(batch * mu_loc, nb))
        hh, hl = split2(dot3(x, (coef_hl[0], coef_hl[1])))
        for u in range(batch):
            at = slice(u * mu_loc, (u + 1) * mu_loc)
            q = dot3((coef_t_hl[0], coef_t_hl[1]), (hh[at], hl[at]))
            t0[pl.ds(p * batch + u, nocc, stride=aux_loc), :] = q[:, :LANES]
            t1[pl.ds(p * batch + u, nocc, stride=aux_loc), :] = q[:, LANES:]
        return carry

    lax.fori_loop(0, n_steps, one_step, 0)

    lane = lax.broadcasted_iota(jnp.int32, (LANES, LANES), 1)

    def one_block(ib):
        for jb, t in enumerate((t0, t1)):
            block = t[pl.ds(pl.multiple_of(ib * LANES, LANES), LANES), :].T
            for g, rep in enumerate(spread(block, lane)):
                at = pl.multiple_of((4 * ib + g) * nocc + jb * LANES, LANES)
                table[pl.ds(at, LANES), :] = rep

    lax.fori_loop(0, nocc // 4, step(one_block), 0)

    row_lane = lax.broadcasted_iota(jnp.int32, (1, LANES), 1) // quarter

    def gather(core, a, out):
        base = (2 * a + core) * (rows_per * 4)

        def some(rb):
            for u in range(16):
                r = rb * 16 + u
                got = [
                    table[pl.ds(rows_ref[owner_ref[base + g * rows_per + r]], 1), :]
                    for g in range(4)
                ]
                low = jnp.where(row_lane == 0, got[0], got[1])
                high = jnp.where(row_lane == 2, got[2], got[3])
                out[a, pl.ds(r, 1), :] = jnp.where(row_lane < 2, low, high)

        lax.fori_loop(0, rows_per // 16, step(some), 0)

    def pair_copy(t):
        a = me_a ^ t
        return pltpu.make_async_remote_copy(
            src_ref=pairs.at[a], dst_ref=pbuf.at[a],
            send_sem=psend.at[t], recv_sem=precv.at[t],
            device_id={"pair": 1 - me_c}, device_id_type=MESH)

    def metric_copy(k, origin):
        to = lax.rem(me + k, n_dev)
        return pltpu.make_async_remote_copy(
            src_ref=metric_ref,
            dst_ref=mfull.at[origin % 2, pl.ds(pl.multiple_of((origin // 2) * q_loc, q_loc), q_loc), :],
            send_sem=msend.at[k], recv_sem=mrecv.at[k],
            device_id={"aux": to // 2, "pair": to % 2}, device_id_type=MESH)

    def aux_copy(t, origin):
        return pltpu.make_async_remote_copy(
            src_ref=snd.at[me_a ^ t], dst_ref=rcv.at[origin],
            send_sem=asend.at[t], recv_sem=arecv.at[t],
            device_id={"aux": me_a ^ t}, device_id_type=MESH)

    pl.semaphore_wait(barrier, n_dev - 1)

    def send(s):
        t = n_aux - 1 - s
        a = me_a ^ t
        gather(1 - me_c, a, pairs)
        pair_copy(t).start()
        gather(me_c, a, snd)
        pair_copy(t).wait_recv()
        snd[a] += pbuf[a]
        aux_copy(t, me_a).start()

    lax.fori_loop(0, n_aux - 1, step(send), 0)
    lax.fori_loop(1, n_dev, step(lambda k: metric_copy(k, me).start()), 0)
    mfull[me_c, pl.ds(pl.multiple_of(me_a * q_loc, q_loc), q_loc), :] = metric_ref[...]
    gather(1 - me_c, me_a, pairs)
    pair_copy(0).start()
    gather(me_c, me_a, snd)
    pair_copy(0).wait_recv()
    rcv[me_a] = snd[me_a] + pbuf[me_a]

    lax.fori_loop(1, n_dev, step(lambda k: metric_copy(k, lax.rem(me + n_dev - k, n_dev)).wait_recv()), 0)

    lane_group = lax.broadcasted_iota(jnp.int32, (rows_per, LANES), 1) // quarter
    blocks = n_aux // 4
    per = blocks // 2
    for s in range(blocks):
        for t in range(4 * s, 4 * s + 4):
            if t > 0:
                aux_copy(t, me_a ^ t).wait_recv()
        b = (me_a // 4) ^ s
        m = split2(mfull[b // per, :, pl.ds(pl.multiple_of((b % per) * LANES, LANES), LANES)])
        for g in range(4):
            y = None
            for u in range(4):
                x = rcv[4 * b + u]
                shift = (quarter * (u - g)) % LANES
                x = pltpu.roll(x, shift, 1) if shift else x
                y = x if y is None else jnp.where(lane_group == u, x, y)
            add = dot3(m, split2(y), (((1,), (1,)), ((), ())))
            if s == 0:
                out_ref[:, g * rows_per:(g + 1) * rows_per] = add
            else:
                out_ref[:, g * rows_per:(g + 1) * rows_per] += add

    lax.fori_loop(0, n_aux, step(lambda t: pair_copy(t).wait_send()), 0)
    lax.fori_loop(1, n_aux, step(lambda t: aux_copy(t, me_a).wait_send()), 0)
    lax.fori_loop(1, n_dev, step(lambda k: metric_copy(k, me).wait_send()), 0)


def body(integrals, coef, screen, domains, owner, metric):
    aux_loc, mu_loc, nb = integrals.shape
    nocc = coef.shape[1]
    n_aux = lax.axis_size("aux")
    dests = 2 * n_aux
    slots = owner.shape[0] // dests
    rows_per = slots // 4
    q_all = metric.shape[0] * n_aux
    rows = (domains + nocc * lax.broadcasted_iota(jnp.int32, domains.shape, 0)).reshape(-1)

    vm = pl.BlockSpec(memory_space=pltpu.VMEM)
    sm = pl.BlockSpec(memory_space=pltpu.SMEM)
    hbm = pl.BlockSpec(memory_space=pl.ANY)
    chunk = pltpu.VMEM((n_aux, rows_per, LANES), jnp.float32)
    half_table = pltpu.VMEM((nocc * aux_loc, LANES), jnp.float32)
    return pl.pallas_call(
        functools.partial(fused_kernel, n_aux),
        out_shape=jax.ShapeDtypeStruct((q_all, slots), jnp.float32),
        in_specs=[hbm, sm, vm, sm, sm, vm],
        out_specs=vm,
        scratch_shapes=[
            pltpu.VMEM((2, BATCH, mu_loc, nb), jnp.float32),
            pltpu.VMEM((mu_loc, nb), jnp.float32),
            pltpu.VMEM((2, nb, nocc), jnp.bfloat16),
            pltpu.VMEM((2, nocc, mu_loc), jnp.bfloat16),
            half_table,
            half_table,
            pltpu.VMEM((nocc * nocc, LANES), jnp.float32),
            chunk,
            chunk,
            chunk,
            chunk,
            pltpu.VMEM((2, q_all, metric.shape[1]), jnp.float32),
            pltpu.SemaphoreType.DMA((2,)),
            pltpu.SemaphoreType.DMA((n_aux,)),
            pltpu.SemaphoreType.DMA((n_aux,)),
            pltpu.SemaphoreType.DMA((n_aux,)),
            pltpu.SemaphoreType.DMA((n_aux,)),
            pltpu.SemaphoreType.DMA((dests,)),
            pltpu.SemaphoreType.DMA((dests,)),
        ],
        compiler_params=pltpu.CompilerParams(
            vmem_limit_bytes=VMEM_LIMIT, collective_id=0, has_side_effects=True),
        name="pair_fit",
    )(integrals, screen, coef, rows, owner, metric)


def solution(mesh):
    placed = (P(("grp", "aux"), "pair", None), P(), P(), P(), P(), P(("grp", "aux"), "pair"))
    return jax.shard_map(
        body, mesh=mesh, in_specs=placed, out_specs=P("grp", ("aux", "pair")), check_vma=False
    )
```

```python
import functools

import jax
import jax.numpy as jnp
from jax import lax
from jax.experimental import pallas as pl
from jax.experimental.pallas import tpu as pltpu
from jax.sharding import PartitionSpec as P

MESH = pl.DeviceIdType.MESH
LANES = 128
BATCH = 4
VMEM_LIMIT = 62 * 1024 * 1024


def split2(x):
    hi = x.astype(jnp.bfloat16)
    lo = (x - hi.astype(jnp.float32)).astype(jnp.bfloat16)
    return hi, lo


def dot3(a, b, dims=(((1,), (0,)), ((), ()))):
    (ah, al), (bh, bl) = a, b
    mm = functools.partial(lax.dot_general, dimension_numbers=dims, preferred_element_type=jnp.float32)
    return mm(ah, bh) + (mm(ah, bl) + mm(al, bh))


def fused_kernel(
    n_aux, integrals_ref, screen_ref, coef_ref, rows_ref, owner_ref, metric_ref, out_ref,
    ibuf, mask, coef_hl, coef_t_hl, t0, t1, table, pairs, pbuf, snd, rcv, mfull,
    sems, psend, precv, asend, arecv, msend, mrecv,
):
    aux_loc, mu_loc, nb = integrals_ref.shape
    nocc = coef_ref.shape[1]
    batch = ibuf.shape[1]
    q_loc = metric_ref.shape[0]
    rows_per = rcv.shape[1]
    n_dev = 2 * n_aux
    me_a = lax.axis_index("aux")
    me_c = lax.axis_index("pair")
    me = 2 * me_a + me_c
    quarter = LANES // 4
    pitch = t0.shape[0] // nocc

    def step(f):
        def g(t, carry):
            f(t)
            return carry
        return g

    barrier = pltpu.get_barrier_semaphore()

    def greet(k):
        to = lax.rem(me + k, n_dev)
        pl.semaphore_signal(barrier, inc=1, device_id={"aux": to // 2, "pair": to % 2}, device_id_type=MESH)

    lax.fori_loop(1, n_dev, step(greet), 0)

    def fetch(p, slot):
        return pltpu.make_async_copy(integrals_ref.at[pl.ds(p * batch, batch)], ibuf.at[slot], sems.at[slot])

    fetch(0, 0).start()
    coef_hl[0], coef_hl[1] = split2(coef_ref[...])
    coef_t = coef_ref[pl.ds(pl.multiple_of(me_c * mu_loc, 64), mu_loc), :].T
    coef_t_hl[0], coef_t_hl[1] = split2(coef_t)
    n_blk = screen_ref.shape[0]
    width = nb // n_blk
    lane_blk = lax.broadcasted_iota(jnp.int32, (width, nb), 1) // width
    for rb in range(mu_loc // width):
        line = jnp.zeros((width, nb), jnp.float32)
        for cb in range(n_blk):
            kept = screen_ref[me_c * (mu_loc // width) + rb, cb].astype(jnp.float32)
            line = jnp.where(lane_blk == cb, kept, line)
        mask[rb * width:(rb + 1) * width, :] = line

    n_steps = aux_loc // batch

    def one_step(p, carry):
        slot = lax.rem(p, 2)

        @pl.when(p + 1 < n_steps)
        def _():
            fetch(p + 1, 1 - slot).start()

        fetch(p, slot).wait()
        x = split2((ibuf[slot] * mask[...][None]).reshape(batch * mu_loc, nb))
        hh, hl = split2(dot3(x, (coef_hl[0], coef_hl[1])))
        for u in range(batch):
            at = slice(u * mu_loc, (u + 1) * mu_loc)
            q = dot3((coef_t_hl[0], coef_t_hl[1]), (hh[at], hl[at]))
            t0[pl.ds(p * batch + u, nocc, stride=pitch), :] = q[:, :LANES]
            t1[pl.ds(p * batch + u, nocc, stride=pitch), :] = q[:, LANES:]
        return carry

    lax.fori_loop(0, n_steps, one_step, 0)

    def one_block(ib):
        for jb, t in enumerate((t0, t1)):
            for g in range(4):
                block = t[pl.ds(pl.multiple_of((4 * ib + g) * pitch, 8), aux_loc), :]
                rep = jnp.concatenate([block] * 4, axis=0).T
                at = pl.multiple_of((4 * ib + g) * nocc + jb * LANES, LANES)
                table[pl.ds(at, LANES), :] = rep

    lax.fori_loop(0, nocc // 4, step(one_block), 0)

    row_lane = lax.broadcasted_iota(jnp.int32, (1, LANES), 1) // quarter

    def gather(core, a, out):
        base = (2 * a + core) * (rows_per * 4)

        def some(rb):
            for u in range(16):
                r = rb * 16 + u
                got = [
                    table[pl.ds(rows_ref[owner_ref[base + g * rows_per + r]], 1), :]
                    for g in range(4)
                ]
                low = jnp.where(row_lane == 0, got[0], got[1])
                high = jnp.where(row_lane == 2, got[2], got[3])
                out[a, pl.ds(r, 1), :] = jnp.where(row_lane < 2, low, high)

        lax.fori_loop(0, rows_per // 16, step(some), 0)

    def pair_copy(t):
        a = me_a ^ t
        return pltpu.make_async_remote_copy(
            src_ref=pairs.at[a], dst_ref=pbuf.at[a],
            send_sem=psend.at[t], recv_sem=precv.at[t],
            device_id={"pair": 1 - me_c}, device_id_type=MESH)

    def metric_copy(k, origin):
        to = lax.rem(me + k, n_dev)
        return pltpu.make_async_remote_copy(
            src_ref=metric_ref,
            dst_ref=mfull.at[origin % 2, pl.ds(pl.multiple_of((origin // 2) * q_loc, q_loc), q_loc), :],
            send_sem=msend.at[k], recv_sem=mrecv.at[k],
            device_id={"aux": to // 2, "pair": to % 2}, device_id_type=MESH)

    def aux_copy(t, origin):
        return pltpu.make_async_remote_copy(
            src_ref=snd.at[me_a ^ t], dst_ref=rcv.at[origin],
            send_sem=asend.at[t], recv_sem=arecv.at[t],
            device_id={"aux": me_a ^ t}, device_id_type=MESH)

    pl.semaphore_wait(barrier, n_dev - 1)

    def send(s):
        t = n_aux - 1 - s
        a = me_a ^ t
        gather(1 - me_c, a, pairs)
        pair_copy(t).start()
        gather(me_c, a, snd)
        pair_copy(t).wait_recv()
        snd[a] += pbuf[a]
        aux_copy(t, me_a).start()

    lax.fori_loop(0, n_aux - 1, step(send), 0)
    lax.fori_loop(1, n_dev, step(lambda k: metric_copy(k, me).start()), 0)
    mfull[me_c, pl.ds(pl.multiple_of(me_a * q_loc, q_loc), q_loc), :] = metric_ref[...]
    gather(1 - me_c, me_a, pairs)
    pair_copy(0).start()
    gather(me_c, me_a, snd)
    pair_copy(0).wait_recv()
    rcv[me_a] = snd[me_a] + pbuf[me_a]

    lax.fori_loop(1, n_dev, step(lambda k: metric_copy(k, lax.rem(me + n_dev - k, n_dev)).wait_recv()), 0)

    lane_group = lax.broadcasted_iota(jnp.int32, (rows_per, LANES), 1) // quarter
    blocks = n_aux // 4
    per = blocks // 2
    for s in range(blocks):
        for t in range(4 * s, 4 * s + 4):
            if t > 0:
                aux_copy(t, me_a ^ t).wait_recv()
        b = (me_a // 4) ^ s
        m = split2(mfull[b // per, :, pl.ds(pl.multiple_of((b % per) * LANES, LANES), LANES)])
        for g in range(4):
            y = None
            for u in range(4):
                x = rcv[4 * b + u]
                shift = (quarter * (u - g)) % LANES
                x = pltpu.roll(x, shift, 1) if shift else x
                y = x if y is None else jnp.where(lane_group == u, x, y)
            add = dot3(m, split2(y), (((1,), (1,)), ((), ())))
            if s == 0:
                out_ref[:, g * rows_per:(g + 1) * rows_per] = add
            else:
                out_ref[:, g * rows_per:(g + 1) * rows_per] += add

    lax.fori_loop(0, n_aux, step(lambda t: pair_copy(t).wait_send()), 0)
    lax.fori_loop(1, n_aux, step(lambda t: aux_copy(t, me_a).wait_send()), 0)
    lax.fori_loop(1, n_dev, step(lambda k: metric_copy(k, me).wait_send()), 0)


def body(integrals, coef, screen, domains, owner, metric):
    aux_loc, mu_loc, nb = integrals.shape
    nocc = coef.shape[1]
    n_aux = lax.axis_size("aux")
    dests = 2 * n_aux
    slots = owner.shape[0] // dests
    rows_per = slots // 4
    q_all = metric.shape[0] * n_aux
    rows = (domains + nocc * lax.broadcasted_iota(jnp.int32, domains.shape, 0)).reshape(-1)

    vm = pl.BlockSpec(memory_space=pltpu.VMEM)
    sm = pl.BlockSpec(memory_space=pltpu.SMEM)
    hbm = pl.BlockSpec(memory_space=pl.ANY)
    chunk = pltpu.VMEM((n_aux, rows_per, LANES), jnp.float32)
    half_table = pltpu.VMEM((nocc * (aux_loc + 8), LANES), jnp.float32)
    return pl.pallas_call(
        functools.partial(fused_kernel, n_aux),
        out_shape=jax.ShapeDtypeStruct((q_all, slots), jnp.float32),
        in_specs=[hbm, sm, vm, sm, sm, vm],
        out_specs=vm,
        scratch_shapes=[
            pltpu.VMEM((2, BATCH, mu_loc, nb), jnp.float32),
            pltpu.VMEM((mu_loc, nb), jnp.float32),
            pltpu.VMEM((2, nb, nocc), jnp.bfloat16),
            pltpu.VMEM((2, nocc, mu_loc), jnp.bfloat16),
            half_table,
            half_table,
            pltpu.VMEM((nocc * nocc, LANES), jnp.float32),
            chunk,
            chunk,
            chunk,
            chunk,
            pltpu.VMEM((2, q_all, metric.shape[1]), jnp.float32),
            pltpu.SemaphoreType.DMA((2,)),
            pltpu.SemaphoreType.DMA((n_aux,)),
            pltpu.SemaphoreType.DMA((n_aux,)),
            pltpu.SemaphoreType.DMA((n_aux,)),
            pltpu.SemaphoreType.DMA((n_aux,)),
            pltpu.SemaphoreType.DMA((dests,)),
            pltpu.SemaphoreType.DMA((dests,)),
        ],
        compiler_params=pltpu.CompilerParams(
            vmem_limit_bytes=VMEM_LIMIT, collective_id=0, has_side_effects=True),
        name="pair_fit",
    )(integrals, screen, coef, rows, owner, metric)


def solution(mesh):
    placed = (P(("grp", "aux"), "pair", None), P(), P(), P(), P(), P(("grp", "aux"), "pair"))
    return jax.shard_map(
        body, mesh=mesh, in_specs=placed, out_specs=P("grp", ("aux", "pair")), check_vma=False
    )
```

```python
import functools

import jax
import jax.numpy as jnp
from jax import lax
from jax.experimental import pallas as pl
from jax.experimental.pallas import tpu as pltpu
from jax.sharding import PartitionSpec as P

MESH = pl.DeviceIdType.MESH
LANES = 128
BATCH = 4
VMEM_LIMIT = 62 * 1024 * 1024


def split2(x):
    hi = x.astype(jnp.bfloat16)
    lo = (x - hi.astype(jnp.float32)).astype(jnp.bfloat16)
    return hi, lo


def dot3(a, b, dims=(((1,), (0,)), ((), ()))):
    (ah, al), (bh, bl) = a, b
    mm = functools.partial(lax.dot_general, dimension_numbers=dims, preferred_element_type=jnp.float32)
    return mm(ah, bh) + (mm(ah, bl) + mm(al, bh))


def fused_kernel(
    n_aux, integrals_ref, screen_ref, coef_ref, rows_ref, owner_ref, metric_ref, out_ref,
    ibuf, mask, coef_hl, coef_t_hl, t0, t1, table, pairs, pbuf, snd, rcv, mfull,
    sems, psend, precv, asend, arecv, msend, mrecv,
):
    aux_loc, mu_loc, nb = integrals_ref.shape
    nocc = coef_ref.shape[1]
    batch = ibuf.shape[1]
    q_loc = metric_ref.shape[0]
    rows_per = rcv.shape[1]
    n_dev = 2 * n_aux
    me_a = lax.axis_index("aux")
    me_c = lax.axis_index("pair")
    me = 2 * me_a + me_c
    quarter = LANES // 4
    pitch = t0.shape[0] // nocc

    def step(f):
        def g(t, carry):
            f(t)
            return carry
        return g

    barrier = pltpu.get_barrier_semaphore()

    def greet(k):
        to = lax.rem(me + k, n_dev)
        pl.semaphore_signal(barrier, inc=1, device_id={"aux": to // 2, "pair": to % 2}, device_id_type=MESH)

    lax.fori_loop(1, n_dev, step(greet), 0)

    def fetch(p, slot):
        return pltpu.make_async_copy(integrals_ref.at[pl.ds(p * batch, batch)], ibuf.at[slot], sems.at[slot])

    fetch(0, 0).start()
    coef_hl[0], coef_hl[1] = split2(coef_ref[...])
    coef_t = coef_ref[pl.ds(pl.multiple_of(me_c * mu_loc, 64), mu_loc), :].T
    coef_t_hl[0], coef_t_hl[1] = split2(coef_t)
    n_blk = screen_ref.shape[0]
    width = nb // n_blk
    lane_blk = lax.broadcasted_iota(jnp.int32, (width, nb), 1) // width
    for rb in range(mu_loc // width):
        line = jnp.zeros((width, nb), jnp.float32)
        for cb in range(n_blk):
            kept = screen_ref[me_c * (mu_loc // width) + rb, cb].astype(jnp.float32)
            line = jnp.where(lane_blk == cb, kept, line)
        mask[rb * width:(rb + 1) * width, :] = line

    n_steps = aux_loc // batch

    def one_step(p, carry):
        slot = lax.rem(p, 2)

        @pl.when(p + 1 < n_steps)
        def _():
            fetch(p + 1, 1 - slot).start()

        fetch(p, slot).wait()
        x = split2((ibuf[slot] * mask[...][None]).reshape(batch * mu_loc, nb))
        hh, hl = split2(dot3(x, (coef_hl[0], coef_hl[1])))
        for u in range(batch):
            at = slice(u * mu_loc, (u + 1) * mu_loc)
            q = dot3((coef_t_hl[0], coef_t_hl[1]), (hh[at], hl[at]))
            t0[pl.ds(p * batch + u, nocc, stride=pitch), :] = q[:, :LANES]
            t1[pl.ds(p * batch + u, nocc, stride=pitch), :] = q[:, LANES:]
        return carry

    lax.fori_loop(0, n_steps, one_step, 0)

    def one_block(ib):
        for jb, t in enumerate((t0, t1)):
            for g in range(4):
                block = t[pl.ds(pl.multiple_of((4 * ib + g) * pitch, 8), aux_loc), :]
                rep = jnp.concatenate([block] * 4, axis=0).T
                at = pl.multiple_of((4 * ib + g) * nocc + jb * LANES, LANES)
                table[pl.ds(at, LANES), :] = rep

    lax.fori_loop(0, nocc // 4, step(one_block), 0)

    row_lane = lax.broadcasted_iota(jnp.int32, (1, LANES), 1) // quarter

    def gather(core, a, out):
        base = (2 * a + core) * (rows_per * 4)

        def some(rb):
            for u in range(16):
                r = rb * 16 + u
                got = [
                    table[pl.ds(rows_ref[owner_ref[base + g * rows_per + r]], 1), :]
                    for g in range(4)
                ]
                low = jnp.where(row_lane == 0, got[0], got[1])
                high = jnp.where(row_lane == 2, got[2], got[3])
                out[a, pl.ds(r, 1), :] = jnp.where(row_lane < 2, low, high)

        lax.fori_loop(0, rows_per // 16, step(some), 0)

    def pair_copy(t):
        a = me_a ^ t
        return pltpu.make_async_remote_copy(
            src_ref=pairs.at[a], dst_ref=pbuf.at[a],
            send_sem=psend.at[t], recv_sem=precv.at[t],
            device_id={"pair": 1 - me_c}, device_id_type=MESH)

    def metric_copy(k, origin):
        to = lax.rem(me + k, n_dev)
        return pltpu.make_async_remote_copy(
            src_ref=metric_ref,
            dst_ref=mfull.at[origin % 2, pl.ds(pl.multiple_of((origin // 2) * q_loc, q_loc), q_loc), :],
            send_sem=msend.at[k], recv_sem=mrecv.at[k],
            device_id={"aux": to // 2, "pair": to % 2}, device_id_type=MESH)

    def aux_copy(t, origin):
        return pltpu.make_async_remote_copy(
            src_ref=snd.at[me_a ^ t], dst_ref=rcv.at[origin],
            send_sem=asend.at[t], recv_sem=arecv.at[t],
            device_id={"aux": me_a ^ t}, device_id_type=MESH)

    pl.semaphore_wait(barrier, n_dev - 1)
    lax.fori_loop(1, n_dev, step(lambda k: metric_copy(k, me).start()), 0)

    def send(s):
        t = (n_aux // 2 + s) % n_aux + s // (n_aux // 2)
        a = me_a ^ t
        gather(1 - me_c, a, pairs)
        pair_copy(t).start()
        gather(me_c, a, snd)
        pair_copy(t).wait_recv()
        snd[a] += pbuf[a]
        aux_copy(t, me_a).start()

    lax.fori_loop(0, n_aux - 1, step(send), 0)
    mfull[me_c, pl.ds(pl.multiple_of(me_a * q_loc, q_loc), q_loc), :] = metric_ref[...]
    gather(1 - me_c, me_a, pairs)
    pair_copy(0).start()
    gather(me_c, me_a, snd)
    pair_copy(0).wait_recv()
    rcv[me_a] = snd[me_a] + pbuf[me_a]

    lax.fori_loop(1, n_dev, step(lambda k: metric_copy(k, lax.rem(me + n_dev - k, n_dev)).wait_recv()), 0)

    lane_group = lax.broadcasted_iota(jnp.int32, (rows_per, LANES), 1) // quarter
    blocks = n_aux // 4
    per = blocks // 2
    for s in range(blocks):
        for t in range(4 * s, 4 * s + 4):
            if t > 0:
                aux_copy(t, me_a ^ t).wait_recv()
        b = (me_a // 4) ^ s
        m = split2(mfull[b // per, :, pl.ds(pl.multiple_of((b % per) * LANES, LANES), LANES)])
        for g in range(4):
            y = None
            for u in range(4):
                x = rcv[4 * b + u]
                shift = (quarter * (u - g)) % LANES
                x = pltpu.roll(x, shift, 1) if shift else x
                y = x if y is None else jnp.where(lane_group == u, x, y)
            add = dot3(m, split2(y), (((1,), (1,)), ((), ())))
            if s == 0:
                out_ref[:, g * rows_per:(g + 1) * rows_per] = add
            else:
                out_ref[:, g * rows_per:(g + 1) * rows_per] += add

    lax.fori_loop(0, n_aux, step(lambda t: pair_copy(t).wait_send()), 0)
    lax.fori_loop(1, n_aux, step(lambda t: aux_copy(t, me_a).wait_send()), 0)
    lax.fori_loop(1, n_dev, step(lambda k: metric_copy(k, me).wait_send()), 0)


def body(integrals, coef, screen, domains, owner, metric):
    aux_loc, mu_loc, nb = integrals.shape
    nocc = coef.shape[1]
    n_aux = lax.axis_size("aux")
    dests = 2 * n_aux
    slots = owner.shape[0] // dests
    rows_per = slots // 4
    q_all = metric.shape[0] * n_aux
    rows = (domains + nocc * lax.broadcasted_iota(jnp.int32, domains.shape, 0)).reshape(-1)

    vm = pl.BlockSpec(memory_space=pltpu.VMEM)
    sm = pl.BlockSpec(memory_space=pltpu.SMEM)
    hbm = pl.BlockSpec(memory_space=pl.ANY)
    chunk = pltpu.VMEM((n_aux, rows_per, LANES), jnp.float32)
    half_table = pltpu.VMEM((nocc * (aux_loc + 8), LANES), jnp.float32)
    return pl.pallas_call(
        functools.partial(fused_kernel, n_aux),
        out_shape=jax.ShapeDtypeStruct((q_all, slots), jnp.float32),
        in_specs=[hbm, sm, vm, sm, sm, vm],
        out_specs=vm,
        scratch_shapes=[
            pltpu.VMEM((2, BATCH, mu_loc, nb), jnp.float32),
            pltpu.VMEM((mu_loc, nb), jnp.float32),
            pltpu.VMEM((2, nb, nocc), jnp.bfloat16),
            pltpu.VMEM((2, nocc, mu_loc), jnp.bfloat16),
            half_table,
            half_table,
            pltpu.VMEM((nocc * nocc, LANES), jnp.float32),
            chunk,
            chunk,
            chunk,
            chunk,
            pltpu.VMEM((2, q_all, metric.shape[1]), jnp.float32),
            pltpu.SemaphoreType.DMA((2,)),
            pltpu.SemaphoreType.DMA((n_aux,)),
            pltpu.SemaphoreType.DMA((n_aux,)),
            pltpu.SemaphoreType.DMA((n_aux,)),
            pltpu.SemaphoreType.DMA((n_aux,)),
            pltpu.SemaphoreType.DMA((dests,)),
            pltpu.SemaphoreType.DMA((dests,)),
        ],
        compiler_params=pltpu.CompilerParams(
            vmem_limit_bytes=VMEM_LIMIT, collective_id=0, has_side_effects=True),
        name="pair_fit",
    )(integrals, screen, coef, rows, owner, metric)


def solution(mesh):
    placed = (P(("grp", "aux"), "pair", None), P(), P(), P(), P(), P(("grp", "aux"), "pair"))
    return jax.shard_map(
        body, mesh=mesh, in_specs=placed, out_specs=P("grp", ("aux", "pair")), check_vma=False
    )
```
